256 devices in a mesh: row: 32 (over x, z), col: 8 (over y, core).
Axes of the slice: x: 4, y: 4, z: 8, core: 2. Of those that a mesh axis runs over, the one named last changes fastest.
Arguments:
- points: float32 [8, 32768], P(None, ('row', 'col')), may hold values from -6 to 6
- length_scales: float32 [8], replicated, may hold values from 1 to 3
- noise: float32 [], replicated, may hold values from 0.5 to 2
- tile_table: int32 [1024], P(('row', 'col')), may hold values from -1 to 31, as said below
- solution: float32 [4, 32768], P(None, ('row', 'col')), may hold values from -6 to 6
- residual: float32 [4, 32768], P(None, ('row', 'col')), may hold values from -6 to 6
- direction: float32 [4, 32768], P(None, ('row', 'col')), may hold values from -6 to 6
Outputs:
- new_solution: float32 [4, 32768], P(None, ('row', 'col'))
- new_residual: float32 [4, 32768], P(None, ('row', 'col'))
- new_direction: float32 [4, 32768], P(None, ('row', 'col'))
The draws below stay inside these ranges and needn't reach their ends.
Inputs may be any that keep to these rules, and one draw needn't show every extreme that they name: `tile_table`: each entry is -1 or a block index above the row block of its device; every pair of blocks appears at most once; some device of row block 0 has all 4 slots filled, and row block 0 lists block 31.
All inputs are finite; a program needn't handle non-finite values.
Results may differ from the reference program's by a relative error of at most 0.0003.
Values sent between devices are 32-bit elements; how exact they have to be, the bound alone decides.
A program may use at most 64 MiB of HBM per device.

```python
import math
import jax
import jax.numpy as jnp
from jax import lax

FEATURES = 8
PROBES = 4
SLOTS = 4
BLOCK = 1024
POINTS = 32768
N_ROW = 32
N_COL = 8


def draw_tile_table(key, part):
    key = jax.random.fold_in(key, 11)
    width = N_COL * SLOTS
    coin_key, col_key, perm_key = jax.random.split(key, 3)
    coin = jax.random.randint(coin_key, (N_ROW, N_ROW), 0, 2)
    rows_idx = jnp.arange(N_ROW, dtype=jnp.int32)[:, None]
    cols_idx = jnp.arange(N_ROW, dtype=jnp.int32)[None, :]
    forced = (rows_idx == 0) & ((cols_idx >= 1) & (cols_idx <= SLOTS) | (cols_idx == N_ROW - 1))
    listed = ((coin == 1) | forced) & (cols_idx > rows_idx)
    ranks = jnp.cumsum(listed.astype(jnp.int32), axis=1) - 1
    full_col = jax.random.randint(col_key, (), 0, N_COL)
    perm_keys = jax.random.split(perm_key, N_ROW)
    perms = jax.vmap(lambda k: jax.random.permutation(k, width))(perm_keys).astype(jnp.int32)
    slot_col = jnp.arange(width, dtype=jnp.int32) // SLOTS
    scores = perms - width * (slot_col == full_col).astype(jnp.int32)[None, :]
    order = jnp.argsort(scores, axis=1, stable=True).astype(jnp.int32)
    target = jnp.take_along_axis(order, jnp.clip(ranks, 0, width - 1), axis=1)
    where_to = jnp.where(listed, target, width)
    partners = jnp.arange(N_ROW, dtype=jnp.int32)

    def fill_row(dest):
        return jnp.full((width,), -1, jnp.int32).at[dest].set(partners, mode='drop')
    return jax.vmap(fill_row)(where_to).reshape(-1)


def shard_levels(key, extent, cuts, smallest, top_value):
    factor_of = 1.0
    for axis_at, parts in cuts:
        heights = jax.random.uniform(jax.random.fold_in(jax.random.fold_in(key, 6), axis_at), (parts,), jnp.float32, smallest / len(cuts), top_value / len(cuts))
        factor_of = factor_of * jnp.repeat(jnp.exp(heights), extent[axis_at] // parts).reshape((-1,) + (1,) * (len(extent) - 1 - axis_at))
    return factor_of


def normal_values(stream_key, dims, scale, limit, cuts=(), held_as=jnp.bfloat16):
    entries = jax.random.normal(stream_key, dims, jnp.float32) * scale
    if len(cuts) > 0:
        entries = shard_levels(stream_key, dims, cuts, -0.22, 0.18) * entries
    return jnp.clip(entries, min=-limit, max=limit).astype(held_as)


def setup_inputs(seed: int = 0) -> dict:
    key_of = jax.random.split(jax.random.key(seed), 8)
    points = normal_values(key_of[0], (FEATURES, POINTS), 1.0, 6.0, ((1, 256),), jnp.float32)
    length_scales = jnp.clip(jnp.exp(jax.random.uniform(key_of[1], (FEATURES,), jnp.float32, math.log(1.0), math.log(3.0))), 1.0, 3.0)
    noise = jnp.clip(jax.random.uniform(key_of[2], (), jnp.float32, 0.5, 2.0), 0.5, 2.0)
    tile_table = draw_tile_table(jax.random.fold_in(key_of[7], 71), 0)
    solution = normal_values(key_of[4], (PROBES, POINTS), 1.0, 6.0, ((1, 256),), jnp.float32)
    residual = normal_values(key_of[5], (PROBES, POINTS), 1.0, 6.0, ((1, 256),), jnp.float32)
    direction = normal_values(key_of[6], (PROBES, POINTS), 1.0, 6.0, ((1, 256),), jnp.float32)
    return {"points": points, "length_scales": length_scales, "noise": noise, "tile_table": tile_table, "solution": solution, "residual": residual, "direction": direction}


root_five = math.sqrt(5.0)

def kernel_tile(left, right, scales):
    first = left / scales[:, None]
    second = right / scales[:, None]
    cross = lax.dot_general(first, second, (((0,), (0,)), ((), ())), precision=lax.Precision.HIGHEST)
    dist_sq = lax.optimization_barrier(jnp.sum(first * first, 0))[:, None] + lax.optimization_barrier(jnp.sum(second * second, 0))[None, :] - 2.0 * cross
    scaled = root_five * jnp.sqrt(jnp.maximum(dist_sq, 0.0))
    return (1.0 + scaled + scaled * scaled / 3.0) * jnp.exp(-scaled)

def times_kernel(vectors, tile):
    return lax.dot_general(vectors, tile, (((1,), (1,)), ((), ())), precision=lax.Precision.HIGHEST)

def reference(points, length_scales, noise, tile_table, solution, residual, direction):
    table = tile_table.reshape(N_ROW, N_COL * SLOTS)
    block_ids = jnp.arange(N_ROW, dtype=jnp.int32)
    listed = jnp.any(table[:, :, None] == block_ids[None, None, :], axis=1).astype(jnp.float32)
    linked = listed + listed.T
    weights = linked + jnp.diag(1.0 + lax.optimization_barrier(jnp.sum(linked, 1)))

    def one_row(index):
        block = lax.dynamic_slice_in_dim(points, (index * BLOCK).astype(jnp.int32), BLOCK, 1)
        tile = kernel_tile(block, points, length_scales)
        row_weight = lax.dynamic_slice_in_dim(weights, index, 1, 0)[0]
        scaled = tile * jnp.repeat(row_weight, BLOCK)[None, :]
        return times_kernel(direction, scaled)
    rows_out = lax.map(one_row, block_ids)
    image = jnp.transpose(rows_out, (1, 0, 2)).reshape(PROBES, POINTS) + noise * direction
    norm_old = lax.optimization_barrier(jnp.sum(residual * residual, 1))
    curv = lax.optimization_barrier(jnp.sum(direction * image, 1))
    alpha = norm_old / curv
    new_solution = solution + alpha[:, None] * direction
    new_residual = residual - alpha[:, None] * image
    norm_new = lax.optimization_barrier(jnp.sum(new_residual * new_residual, 1))
    new_direction = new_residual + (norm_new / norm_old)[:, None] * direction
    return (new_solution, new_residual, new_direction)
```

```python
import math

import jax
import jax.numpy as jnp
from jax import lax
from jax.experimental import pallas as pl
from jax.experimental.pallas import tpu as pltpu
from jax.sharding import PartitionSpec as P

F32, BF16 = jnp.float32, jnp.bfloat16
MESH = pl.DeviceIdType.MESH
ROOT3 = math.sqrt(3.0)
RATE = -ROOT3 * math.log2(math.e)
POINT_SCALE = math.sqrt(5.0 / 3.0)
NX, NY, NZ, NC = 4, 4, 8, 2
GROUP = 16
W = 128
DEPTH = 64


def split3(a):
    high = a.astype(BF16).astype(F32)
    rest = a - high
    mid = rest.astype(BF16).astype(F32)
    return high, mid, rest - mid


def norm_rows(a, first):
    n = split3(jnp.sum(a * a, axis=0, keepdims=True))
    row = lax.broadcasted_iota(jnp.int32, a.shape, 0)
    at = 0 if first else 3
    ones = ((row >= 3 - at) & (row < 6 - at)).astype(F32)
    for k in range(3):
        ones = jnp.where(row == at + k, n[k], ones)
    return ones


def right_rows(a):
    h, m, l = split3(a)
    return jnp.concatenate([h, h, h, m, m, l, norm_rows(a, False), jnp.zeros_like(a)], 0)


def left_rows(a):
    h, m, l = (-2.0 * part for part in split3(a))
    return jnp.concatenate([h, m, l, h, m, h, norm_rows(a, True), jnp.zeros_like(a)], 0)


def kern_of(s):
    s = jnp.maximum(s, 1e-30)
    v = s * lax.rsqrt(s)
    return ((v + ROOT3) * v + 1.0) * jnp.exp2(v * RATE)


def body(
    scales, noise, table, points, sol, res, dirs, new_sol, new_res, new_dir,
    pbuf, qbuf, tbuf, rbuf, s1buf, s2buf, sendr, left, right, dlhs, acc, wbuf,
    p_recv, q_recv, t_recv, r_recv, s1_recv, s2_recv, send_sem,
):
    row, col = lax.axis_index("row"), lax.axis_index("col")
    x, z = lax.div(row, NZ), lax.rem(row, NZ)
    y, core = lax.div(col, NC), lax.rem(col, NC)

    def p_at(k, sign):
        zz = lax.rem(z + (sign * (k % NZ)) % NZ, NZ)
        cc = lax.rem(core + k // NZ, NC)
        return (x * NZ + zz, y * NC + cc)

    def q_at(m, sign):
        xx = lax.rem(x + (sign * (m // NY)) % NX, NX)
        yy = lax.rem(y + (sign * (m % NY)) % NY, NY)
        return (xx * NZ + z, yy * NC + core)

    others = range(1, GROUP)
    barrier = pltpu.get_barrier_semaphore()
    for k in others:
        pl.semaphore_signal(barrier, inc=1, device_id=p_at(k, 1), device_id_type=MESH)
        pl.semaphore_signal(barrier, inc=1, device_id=q_at(k, 1), device_id_type=MESH)

    sub = lax.broadcasted_iota(jnp.int32, (8, W), 0)
    lane = lax.broadcasted_iota(jnp.int32, (8, W), 1)
    col_scale = jnp.full((8, W), scales[0], F32)
    for f in range(1, 8):
        col_scale = jnp.where(sub == f, scales[f], col_scale)
    a = points[...] / col_scale * POINT_SCALE
    pbuf[0] = a
    lane1 = lax.broadcasted_iota(jnp.int32, (1, W), 1)
    own_table = jnp.full((1, W), table[0].astype(F32), F32)
    for s in range(1, 4):
        own_table = jnp.where(lax.rem(lane1, 4) == s, table[s].astype(F32), own_table)
    qbuf[0, 0:8] = a
    qbuf[0, 8:12] = dirs[...]
    qbuf[0, 12:16] = jnp.broadcast_to(own_table, (4, W))

    def p_copy(src, buf, recv, k, sem, sign=1):
        return pltpu.make_async_remote_copy(
            src_ref=src, dst_ref=buf.at[k], send_sem=send_sem.at[sem, k], recv_sem=recv.at[k],
            device_id=p_at(k, sign), device_id_type=MESH,
        )

    def q_copy(src, buf, recv, k, sem):
        return pltpu.make_async_remote_copy(
            src_ref=src, dst_ref=buf.at[k], send_sem=send_sem.at[sem, k], recv_sem=recv.at[k],
            device_id=q_at(k, 1), device_id_type=MESH,
        )

    pl.semaphore_wait(barrier, 2 * (GROUP - 1))
    p_copies = {k: p_copy(pbuf.at[0], pbuf, p_recv, k, 0) for k in others}
    q_copies = {k: q_copy(qbuf.at[0], qbuf, q_recv, k, 1) for k in others}
    for k in others:
        p_copies[k].start()
        q_copies[k].start()

    def prep_right(k):
        right[:, pl.ds(k * W, W)] = right_rows(pbuf[k]).astype(BF16)

    def prep_left(m):
        left[pl.ds(m * W, W), :] = left_rows(qbuf[m, 0:8]).T.astype(BF16)
        h, mid, low = split3(qbuf[m, 8:12])
        dlhs[:, pl.ds(m * W, W)] = jnp.concatenate([h, mid, low, jnp.zeros_like(h)], 0).astype(BF16)

    def tile(pair, mx, first, ppair):
        q0, p0 = pair * 256, ppair * 256
        s = jnp.dot(left[pl.ds(q0, 256), :], right[:, pl.ds(p0, 256)], preferred_element_type=F32)
        kern = kern_of(s)
        high = kern.astype(BF16)
        low = (kern - high.astype(F32)).astype(BF16)
        d = dlhs[:, pl.ds(q0, 256)]
        both = jnp.dot(d, high, preferred_element_type=F32)
        both += jnp.dot(d, low, preferred_element_type=F32)
        at = (mx, slice(None), pl.ds(p0, 256))
        acc[at] = both if first else acc[at] + both

    prep_right(0)
    prep_left(0)
    for k in others:
        p_copies[k].wait_recv()
        prep_right(k)
    for pair in range(8):
        for m in (2 * pair, 2 * pair + 1):
            if m > 0:
                q_copies[m].wait_recv()
                prep_left(m)
        for ppair in range(8):
            tile(pair, pair // 2, pair % 2 == 0, ppair)

    joined = jnp.where(lane1 < 4, qbuf[0, 12:13], -1.0)
    for m in others:
        joined = jnp.where(lax.div(lane1, 4) == m, qbuf[m, 12:13], joined)
    tbuf[0] = joined
    t_copies = {k: p_copy(tbuf.at[0], tbuf, t_recv, k, 2) for k in others}
    for k in others:
        t_copies[k].start()
    for k in others:
        t_copies[k].wait_recv()

    tt = [jnp.concatenate([tbuf[kc * NZ + kz] for kz in range(NZ)], 0) for kc in range(NC)]
    rp = (x * NZ + lax.rem(z + NZ - sub, NZ)).astype(F32)
    own = row.astype(F32)
    far = sum((jnp.broadcast_to(t[0:1], (8, W)) == rp).astype(F32) for t in tt)
    degree = sum(
        jnp.where((t == own) | ((t >= 0.0) & (lane < 16) & (sub == 0)), 1.0, 0.0) for t in tt
    )
    degree = jnp.sum(jnp.sum(degree, axis=1, keepdims=True), axis=0, keepdims=True)
    for mx in range(NX):
        rq = (lax.rem(x + NX - mx, NX) * NZ + z).astype(F32)
        listed = jnp.where(lax.div(lane, 16) == mx, far, 0.0)
        listed += sum(((t == rq) & (lane < 16)).astype(F32) for t in tt)
        weight = jnp.broadcast_to(jnp.sum(listed, axis=1, keepdims=True), (8, W))
        if mx == 0:
            weight = jnp.where(sub == 0, 1.0 + degree, weight)
        wbuf[mx] = weight

    def partial(k):
        total = jnp.zeros((4, W), F32)
        for mx in range(NX):
            at = pl.ds(k * W, W)
            part = acc[mx, 0:4, at] + (acc[mx, 4:8, at] + acc[mx, 8:12, at])
            total += part * wbuf[mx, pl.ds(k % NZ, 1), :]
        return total

    r_copies = {k: p_copy(sendr.at[k], rbuf, r_recv, k, 3, -1) for k in others}
    for k in others:
        sendr[k] = partial(k)
        r_copies[k].start()
    d = dirs[...]
    image = partial(0) + noise[0] * d
    for k in others:
        r_copies[k].wait_recv()
        image += rbuf[k]

    r = res[...]
    parts = jnp.concatenate([r * r, d * image, r * image, image * image], 0)
    sums = jnp.sum(parts, axis=1, keepdims=True)
    sub16 = lax.broadcasted_iota(jnp.int32, (16, W), 0)
    lane16 = lax.broadcasted_iota(jnp.int32, (16, W), 1)

    s1buf[0] = jnp.sum(jnp.where(sub16 == lane16, sums, 0.0), axis=0, keepdims=True)
    s1_copies = {k: p_copy(s1buf.at[0], s1buf, s1_recv, k, 4) for k in others}
    for k in others:
        s1_copies[k].start()
    for k in others:
        s1_copies[k].wait_recv()
    s2buf[0] = jnp.sum(s1buf[...], axis=0)
    s2_copies = {k: q_copy(s2buf.at[0], s2buf, s2_recv, k, 5) for k in others}
    for k in others:
        s2_copies[k].start()
    for k in others:
        s2_copies[k].wait_recv()
    total = jnp.sum(s2buf[...], axis=0)
    sums = jnp.sum(jnp.where(sub16 == lane16, total, 0.0), axis=1, keepdims=True)
    rr, curv, ri, ii = (sums[4 * i : 4 * i + 4] for i in range(4))
    alpha = rr / curv
    rr_new = jnp.maximum(rr - alpha * (2.0 * ri - alpha * ii), 0.0)
    beta = rr_new / rr
    nr = r - alpha * image
    new_sol[...] = sol[...] + alpha * d
    new_res[...] = nr
    new_dir[...] = nr + beta * d
    for copies in (p_copies, q_copies, t_copies, r_copies, s1_copies, s2_copies):
        for k in others:
            copies[k].wait_send()


def local(points, length_scales, noise, tile_table, solution, residual, direction):
    vmem = pl.BlockSpec(memory_space=pltpu.VMEM)
    smem = pl.BlockSpec(memory_space=pltpu.SMEM)
    out = jax.ShapeDtypeStruct(direction.shape, F32)
    dma = pltpu.SemaphoreType.DMA
    return pl.pallas_call(
        body,
        out_shape=(out, out, out),
        in_specs=[smem, smem, smem, vmem, vmem, vmem, vmem],
        out_specs=(vmem, vmem, vmem),
        scratch_shapes=[
            pltpu.VMEM((GROUP, 8, W), F32),
            pltpu.VMEM((GROUP, 16, W), F32),
            pltpu.VMEM((GROUP, 1, W), F32),
            pltpu.VMEM((GROUP, 4, W), F32),
            pltpu.VMEM((GROUP, 1, W), F32),
            pltpu.VMEM((GROUP, 1, W), F32),
            pltpu.VMEM((GROUP, 4, W), F32),
            pltpu.VMEM((GROUP * W, DEPTH), BF16),
            pltpu.VMEM((DEPTH, GROUP * W), BF16),
            pltpu.VMEM((16, GROUP * W), BF16),
            pltpu.VMEM((NX, 16, GROUP * W), F32),
            pltpu.VMEM((NX, 8, W), F32),
        ]
        + [dma((GROUP,))] * 6
        + [dma((6, GROUP))],
        compiler_params=pltpu.CompilerParams(
            collective_id=0, has_side_effects=True, vmem_limit_bytes=40 * 2**20
        ),
    )(length_scales, noise.reshape(1), tile_table, points, solution, residual, direction)


def solution(mesh):
    vec = P(None, ("row", "col"))
    return jax.shard_map(
        local,
        mesh=mesh,
        in_specs=(vec, P(), P(), P(("row", "col")), vec, vec, vec),
        out_specs=(vec, vec, vec),
        check_vma=False,
    )
```

```python
import math

import jax
import jax.numpy as jnp
from jax import lax
from jax.experimental import pallas as pl
from jax.experimental.pallas import tpu as pltpu
from jax.sharding import PartitionSpec as P

F32, BF16 = jnp.float32, jnp.bfloat16
MESH = pl.DeviceIdType.MESH
ROOT3 = math.sqrt(3.0)
RATE = -ROOT3 * math.log2(math.e)
POINT_SCALE = math.sqrt(5.0 / 3.0)
NX, NY, NZ, NC = 4, 4, 8, 2
CHIPS = NX * NY * NZ
GROUP = 16
W = 128
DEPTH = 64


def split3(a):
    high = a.astype(BF16).astype(F32)
    rest = a - high
    mid = rest.astype(BF16).astype(F32)
    return high, mid, rest - mid


def norm_rows(a, first):
    n = split3(jnp.sum(a * a, axis=0, keepdims=True))
    row = lax.broadcasted_iota(jnp.int32, a.shape, 0)
    at = 0 if first else 3
    ones = ((row >= 3 - at) & (row < 6 - at)).astype(F32)
    for k in range(3):
        ones = jnp.where(row == at + k, n[k], ones)
    return ones


def right_rows(a):
    h, m, l = split3(a)
    return jnp.concatenate([h, h, h, m, m, l, norm_rows(a, False), jnp.zeros_like(a)], 0)


def left_rows(a):
    h, m, l = (-2.0 * part for part in split3(a))
    return jnp.concatenate([h, m, l, h, m, h, norm_rows(a, True), jnp.zeros_like(a)], 0)


def kern_of(s):
    s = jnp.maximum(s, 1e-30)
    v = s * lax.rsqrt(s)
    return ((v + ROOT3) * v + 1.0) * jnp.exp2(v * RATE)


def body(
    scales_in, noise_in, table_in, points_in, sol_in, res_in, dirs_in, out,
    scales, noise, table, points, sol, res, dirs,
    pbuf, qbuf, tbuf, rbuf, s1buf, s2buf, sendr, left, right, dlhs, acc,
    in_sem, p_recv, q_recv, t_recv, r_recv, s1_recv, s2_recv, send_sem,
):
    row, col = lax.axis_index("row"), lax.axis_index("col")
    x, z = lax.div(row, NZ), lax.rem(row, NZ)
    y, core = lax.div(col, NC), lax.rem(col, NC)

    def p_at(k, sign):
        zz = lax.rem(z + (sign * (k // NC)) % NZ, NZ)
        cc = lax.rem(core + k % NC, NC)
        return (x * NZ + zz, y * NC + cc)

    def q_at(m, sign):
        xx = lax.rem(x + (sign * (m // NY)) % NX, NX)
        yy = lax.rem(y + (sign * (m % NY)) % NY, NY)
        return (xx * NZ + z, yy * NC + core)

    loads = [
        pltpu.make_async_copy(src, dst, in_sem.at[i])
        for i, (src, dst) in enumerate(
            (
                (points_in, points), (scales_in, scales), (table_in, table), (dirs_in, dirs),
                (noise_in, noise), (sol_in, sol), (res_in, res),
            )
        )
    ]
    others = range(1, GROUP)
    barrier = pltpu.get_barrier_semaphore()
    for k in others:
        pl.semaphore_signal(barrier, inc=1, device_id=p_at(k, 1), device_id_type=MESH)
        pl.semaphore_signal(barrier, inc=1, device_id=q_at(k, 1), device_id_type=MESH)

    for load in loads:
        load.start()
    sub = lax.broadcasted_iota(jnp.int32, (8, W), 0)
    lane = lax.broadcasted_iota(jnp.int32, (8, W), 1)
    for load in loads[:5]:
        load.wait()
    col_scale = jnp.full((8, W), scales[0], F32)
    for f in range(1, 8):
        col_scale = jnp.where(sub == f, scales[f], col_scale)
    a = points[...] / col_scale * POINT_SCALE
    pbuf[0] = a
    lane1 = lax.broadcasted_iota(jnp.int32, (1, W), 1)
    own_table = jnp.full((1, W), table[0].astype(F32), F32)
    for s in range(1, 4):
        own_table = jnp.where(lax.rem(lane1, 4) == s, table[s].astype(F32), own_table)
    qbuf[0, 0:8] = a
    qbuf[0, 8:12] = dirs[...]
    qbuf[0, 12:16] = jnp.broadcast_to(own_table, (4, W))

    def p_copy(src, buf, recv, k, sem, sign=1):
        return pltpu.make_async_remote_copy(
            src_ref=src, dst_ref=buf.at[k], send_sem=send_sem.at[sem, k], recv_sem=recv.at[k],
            device_id=p_at(k, sign), device_id_type=MESH,
        )

    def q_copy(src, buf, recv, k, sem):
        return pltpu.make_async_remote_copy(
            src_ref=src, dst_ref=buf.at[k], send_sem=send_sem.at[sem, k], recv_sem=recv.at[k],
            device_id=q_at(k, 1), device_id_type=MESH,
        )

    pl.semaphore_wait(barrier, 2 * (GROUP - 1))
    p_copies = {k: p_copy(pbuf.at[0], pbuf, p_recv, k, 0) for k in others}
    q_copies = {k: q_copy(qbuf.at[0], qbuf, q_recv, k, 1) for k in others}
    for k in others:
        p_copies[k].start()
        q_copies[k].start()

    def prep_right(k):
        right[:, pl.ds(k * W, W)] = right_rows(pbuf[k]).astype(BF16)

    def prep_left(m):
        left[pl.ds(m * W, W), :] = left_rows(qbuf[m, 0:8]).T.astype(BF16)
        h, mid, low = split3(qbuf[m, 8:12])
        dlhs[:, pl.ds(m * W, W)] = jnp.concatenate([h, mid, low, jnp.zeros_like(h)], 0).astype(BF16)

    def tile(pair, mx, first, ppair):
        q0, p0 = pair * 256, ppair * 256
        s = jnp.dot(left[pl.ds(q0, 256), :], right[:, pl.ds(p0, 256)], preferred_element_type=F32)
        kern = kern_of(s)
        high = kern.astype(BF16)
        low = (kern - high.astype(F32)).astype(BF16)
        d = dlhs[:, pl.ds(q0, 256)]
        both = jnp.dot(d, high, preferred_element_type=F32)
        both += jnp.dot(d, low, preferred_element_type=F32)
        at = (mx, slice(None), pl.ds(p0, 256))
        acc[at] = both if first else acc[at] + both

    def arrive_p(*pairs):
        for pair in pairs:
            for k in (2 * pair, 2 * pair + 1):
                if k > 0:
                    p_copies[k].wait_recv()
                prep_right(k)

    def arrive_q(*pairs):
        for pair in pairs:
            for m in (2 * pair, 2 * pair + 1):
                if m > 0:
                    q_copies[m].wait_recv()
                prep_left(m)

    def region(step):
        pl.when(row >= 0)(step)

    done = set()

    def tiles(ppairs, pairs):
        for ppair in ppairs:
            for pair in pairs:
                if (ppair, pair) not in done:
                    first = (ppair, pair ^ 1) not in done
                    tile(pair, pair // 2, first, ppair)
                    done.add((ppair, pair))

    @region
    def _():
        arrive_p(0, 1, 7)
        arrive_q(0)
        tiles((0, 1, 7), (0,))

    @region
    def _():
        arrive_q(1, 2, 6)
        tiles((0, 1, 7), (1, 2, 6))

    @region
    def _():
        arrive_p(2, 6)
        tiles((2, 6), (0, 1, 2, 6))

    arrive_p(3, 5, 4)
    arrive_q(3, 7, 4, 5)

    joined = jnp.where(lane1 < 4, qbuf[0, 12:13], -1.0)
    for m in others:
        joined = jnp.where(lax.div(lane1, 4) == m, qbuf[m, 12:13], joined)
    tbuf[0] = joined
    t_copies = {k: p_copy(tbuf.at[0], tbuf, t_recv, k, 2) for k in others}
    for k in others:
        t_copies[k].start()

    r_copies = {k: p_copy(sendr.at[k], rbuf, r_recv, k, 3, -1) for k in others}
    def finish(ppairs):
        tiles(ppairs, range(8))
        for k in (2 * p + kc for p in ppairs for kc in range(NC)):
            for mx in range(NX):
                at = pl.ds(k * W, W)
                sendr[k, 4 * mx : 4 * mx + 4] = acc[mx, 0:4, at] + (
                    acc[mx, 4:8, at] + acc[mx, 8:12, at]
                )
            if k > 0:
                r_copies[k].start()

    region(lambda: finish((4, 3, 5)))
    region(lambda: finish((2, 6)))
    region(lambda: finish((1, 7, 0)))

    for k in others:
        t_copies[k].wait_recv()

    sub16 = lax.broadcasted_iota(jnp.int32, (16, W), 0)
    lane16 = lax.broadcasted_iota(jnp.int32, (16, W), 1)
    group = lax.div(sub16, 4)
    tt = [jnp.concatenate([tbuf[2 * kz + kc] for kz in range(NZ)], 0) for kc in range(NC)]
    own = row.astype(F32)
    lists_me = sum((t == own).astype(F32) for t in tt)
    degree = lists_me + sum(
        jnp.where((t >= 0.0) & (lane < 16) & (sub == 0), 1.0, 0.0) for t in tt
    )
    degree = jnp.sum(jnp.sum(degree, axis=1, keepdims=True), axis=0, keepdims=True)
    mine = [jnp.where(lane1 < 16, t[0:1], -1.0) for t in tt]
    d = dirs[...]
    weighted = jnp.zeros((16, W), F32)
    for kz in (4, 3, 5, 2, 6, 1, 7, 0):
        at = (NZ - kz) % NZ
        block = (lax.rem(x + NX - group, NX) * NZ + lax.rem(z + kz, NZ)).astype(F32)
        linked = jnp.where(lax.div(lane16, 16) == group, lists_me[at : at + 1], 0.0)
        linked += sum((t == block).astype(F32) for t in mine)
        weight = jnp.sum(linked, axis=1, keepdims=True)
        if kz == 0:
            weight = jnp.where(sub16[:, 0:1] < 4, 1.0 + degree, weight)
        for k in (2 * kz, 2 * kz + 1):
            if k > 0:
                r_copies[k].wait_recv()
            weighted += weight * (rbuf[k] if k > 0 else sendr[0])
    image = sum(weighted[4 * mx : 4 * mx + 4] for mx in range(NX)) + noise[0] * d

    loads[5].wait()
    loads[6].wait()
    r = res[...]
    parts = jnp.concatenate([r * r, d * image, r * image, image * image], 0)
    sums = jnp.sum(parts, axis=1, keepdims=True)
    s1buf[0] = jnp.sum(jnp.where(sub16 == lane16, sums, 0.0), axis=0, keepdims=True)
    pair_copy = p_copy(s1buf.at[0], s1buf, s1_recv, 1, 4)
    pair_copy.start()
    pair_copy.wait_recv()
    s2buf[0] = s1buf[0] + s1buf[1]

    xs = [lax.rem(x + d, NX) * NZ for d in range(NX)]
    ys = [lax.rem(y + d, NY) * NC + core for d in range(NY)]
    zs = [lax.rem(z + d, NZ) for d in range(NZ)]

    def hops(slot):
        at = ((slot // 32, NX), (slot // 8 % 4, NY), (slot % 8, NZ))
        return sum(min(d, extent - d) for d, extent in at)

    for slot in sorted(range(1, CHIPS), key=hops, reverse=True):
        pltpu.make_async_remote_copy(
            src_ref=s2buf.at[0], dst_ref=s2buf.at[slot],
            send_sem=send_sem.at[5, 0], recv_sem=s2_recv.at[0],
            device_id=(xs[slot // 32] + zs[slot % 8], ys[slot // 8 % 4]), device_id_type=MESH,
        ).start()
    rest = s2buf.at[pl.ds(1, CHIPS - 1)]
    pltpu.make_async_copy(rest, rest, s2_recv.at[0]).wait()
    total = jnp.sum(s2buf[...], axis=0)
    sums = jnp.sum(jnp.where(sub16 == lane16, total, 0.0), axis=1, keepdims=True)
    rr, curv, ri, ii = (sums[4 * i : 4 * i + 4] for i in range(4))
    alpha = rr / curv
    rr_new = jnp.maximum(rr - alpha * (2.0 * ri - alpha * ii), 0.0)
    beta = rr_new / rr
    nr = r - alpha * image
    out[0:4] = sol[...] + alpha * d
    out[4:8] = nr
    out[8:12] = nr + beta * d
    pair_copy.wait_send()
    pltpu.make_async_copy(rest, rest, send_sem.at[5, 0]).wait()
    for copies in (p_copies, q_copies, t_copies, r_copies):
        for k in others:
            copies[k].wait_send()


def local(points, length_scales, noise, tile_table, solution, residual, direction):
    hbm = pl.BlockSpec(memory_space=pltpu.HBM)
    dma = pltpu.SemaphoreType.DMA
    out = pl.pallas_call(
        body,
        out_shape=jax.ShapeDtypeStruct((12, W), F32),
        in_specs=[hbm] * 7,
        out_specs=pl.BlockSpec(memory_space=pltpu.VMEM),
        scratch_shapes=[
            pltpu.SMEM((8,), F32),
            pltpu.SMEM((1,), F32),
            pltpu.SMEM((4,), jnp.int32),
            pltpu.VMEM((8, W), F32),
            pltpu.VMEM((4, W), F32),
            pltpu.VMEM((4, W), F32),
            pltpu.VMEM((4, W), F32),
            pltpu.VMEM((GROUP, 8, W), F32),
            pltpu.VMEM((GROUP, 16, W), F32),
            pltpu.VMEM((GROUP, 1, W), F32),
            pltpu.VMEM((GROUP, 16, W), F32),
            pltpu.VMEM((2, 1, W), F32),
            pltpu.VMEM((CHIPS, 1, W), F32),
            pltpu.VMEM((GROUP, 16, W), F32),
            pltpu.VMEM((GROUP * W, DEPTH), BF16),
            pltpu.VMEM((DEPTH, GROUP * W), BF16),
            pltpu.VMEM((16, GROUP * W), BF16),
            pltpu.VMEM((NX, 16, GROUP * W), F32),
            dma((7,)),
        ]
        + [dma((GROUP,))] * 6
        + [dma((6, GROUP))],
        compiler_params=pltpu.CompilerParams(
            collective_id=0, has_side_effects=True, vmem_limit_bytes=64 * 2**20 - 65536
        ),
    )(length_scales, noise.reshape(1), tile_table, points, solution, residual, direction)
    return out[0:4], out[4:8], out[8:12]


def solution(mesh):
    vec = P(None, ("row", "col"))
    return jax.shard_map(
        local,
        mesh=mesh,
        in_specs=(vec, P(), P(), P(("row", "col")), vec, vec, vec),
        out_specs=(vec, vec, vec),
        check_vma=False,
    )
```

```python
import math

import jax
import jax.numpy as jnp
from jax import lax
from jax.experimental import pallas as pl
from jax.experimental.pallas import tpu as pltpu
from jax.sharding import PartitionSpec as P

F32, BF16 = jnp.float32, jnp.bfloat16
MESH = pl.DeviceIdType.MESH
ROOT3 = math.sqrt(3.0)
RATE = -ROOT3 * math.log2(math.e)
POINT_SCALE = math.sqrt(5.0 / 3.0)
NX, NY, NZ, NC = 4, 4, 8, 2
CHIPS = NX * NY * NZ
GROUP = 16
W = 128
DEPTH = 64


def split3(a):
    high = a.astype(BF16).astype(F32)
    rest = a - high
    mid = rest.astype(BF16).astype(F32)
    return high, mid, rest - mid


def norm_rows(a, first):
    n = split3(jnp.sum(a * a, axis=0, keepdims=True))
    row = lax.broadcasted_iota(jnp.int32, a.shape, 0)
    at = 0 if first else 3
    ones = ((row >= 3 - at) & (row < 6 - at)).astype(F32)
    for k in range(3):
        ones = jnp.where(row == at + k, n[k], ones)
    return ones


def right_rows(a):
    h, m, l = split3(a)
    return jnp.concatenate([h, h, h, m, m, l, norm_rows(a, False), jnp.zeros_like(a)], 0)


def left_rows(a):
    h, m, l = (-2.0 * part for part in split3(a))
    return jnp.concatenate([h, m, l, h, m, h, norm_rows(a, True), jnp.zeros_like(a)], 0)


def kern_of(s):
    s = jnp.maximum(s, 1e-30)
    v = s * lax.rsqrt(s)
    return (s + (ROOT3 * v + 1.0)) * jnp.exp2(v * RATE)


def body(
    scales_in, noise_in, table_in, points_in, sol_in, res_in, dirs_in, out,
    scales, noise, table, points, sol, res, dirs,
    pbuf, qbuf, tbuf, rbuf, s1buf, s2buf, sendr, left, right, dlhs, acc,
    in_sem, p_recv, q_recv, t_recv, r_recv, s1_recv, s2_recv, send_sem,
):
    row, col = lax.axis_index("row"), lax.axis_index("col")
    x, z = lax.div(row, NZ), lax.rem(row, NZ)
    y, core = lax.div(col, NC), lax.rem(col, NC)

    def p_at(k, sign):
        zz = lax.rem(z + (sign * (k // NC)) % NZ, NZ)
        cc = lax.rem(core + k % NC, NC)
        return (x * NZ + zz, y * NC + cc)

    def q_at(m, sign):
        xx = lax.rem(x + (sign * (m // NY)) % NX, NX)
        yy = lax.rem(y + (sign * (m % NY)) % NY, NY)
        return (xx * NZ + z, yy * NC + core)

    loads = [
        pltpu.make_async_copy(src, dst, in_sem.at[i])
        for i, (src, dst) in enumerate(
            (
                (points_in, points), (scales_in, scales), (table_in, table), (dirs_in, dirs),
                (noise_in, noise), (sol_in, sol), (res_in, res),
            )
        )
    ]
    others = range(1, GROUP)
    barrier = pltpu.get_barrier_semaphore()
    for k in others:
        pl.semaphore_signal(barrier, inc=1, device_id=p_at(k, 1), device_id_type=MESH)
        pl.semaphore_signal(barrier, inc=1, device_id=q_at(k, 1), device_id_type=MESH)

    for load in loads:
        load.start()
    sub = lax.broadcasted_iota(jnp.int32, (8, W), 0)
    lane = lax.broadcasted_iota(jnp.int32, (8, W), 1)
    for load in loads[:5]:
        load.wait()
    col_scale = jnp.full((8, W), scales[0], F32)
    for f in range(1, 8):
        col_scale = jnp.where(sub == f, scales[f], col_scale)
    a = points[...] / col_scale * POINT_SCALE
    pbuf[0] = a
    lane1 = lax.broadcasted_iota(jnp.int32, (1, W), 1)
    own_table = jnp.full((1, W), table[0].astype(F32), F32)
    for s in range(1, 4):
        own_table = jnp.where(lax.rem(lane1, 4) == s, table[s].astype(F32), own_table)
    qbuf[0, 0:8] = a
    qbuf[0, 8:12] = dirs[...]
    qbuf[0, 12:16] = jnp.broadcast_to(own_table, (4, W))

    def p_copy(src, buf, recv, k, sem, sign=1):
        return pltpu.make_async_remote_copy(
            src_ref=src, dst_ref=buf.at[k], send_sem=send_sem.at[sem, k], recv_sem=recv.at[k],
            device_id=p_at(k, sign), device_id_type=MESH,
        )

    def q_copy(src, buf, recv, k, sem):
        return pltpu.make_async_remote_copy(
            src_ref=src, dst_ref=buf.at[k], send_sem=send_sem.at[sem, k], recv_sem=recv.at[k],
            device_id=q_at(k, 1), device_id_type=MESH,
        )

    pl.semaphore_wait(barrier, 2 * (GROUP - 1))
    p_copies = {k: p_copy(pbuf.at[0], pbuf, p_recv, k, 0) for k in others}
    q_copies = {k: q_copy(qbuf.at[0], qbuf, q_recv, k, 1) for k in others}
    for k in others:
        p_copies[k].start()
        q_copies[k].start()

    def prep_right(k):
        right[:, pl.ds(k * W, W)] = right_rows(pbuf[k]).astype(BF16)

    def prep_left(m):
        left[pl.ds(m * W, W), :] = left_rows(qbuf[m, 0:8]).T.astype(BF16)
        h, mid, low = split3(qbuf[m, 8:12])
        dlhs[:, pl.ds(m * W, W)] = jnp.concatenate([h, mid, low, jnp.zeros_like(h)], 0).astype(BF16)

    def tile(pair, mx, first, ppair):
        q0, p0 = pair * 256, ppair * 256
        s = jnp.dot(left[pl.ds(q0, 256), :], right[:, pl.ds(p0, 256)], preferred_element_type=F32)
        kern = kern_of(s)
        high = kern.astype(BF16)
        low = (kern - high.astype(F32)).astype(BF16)
        d = dlhs[:, pl.ds(q0, 256)]
        both = jnp.dot(d, high, preferred_element_type=F32)
        both += jnp.dot(d, low, preferred_element_type=F32)
        at = (mx, slice(None), pl.ds(p0, 256))
        acc[at] = both if first else acc[at] + both

    def arrive_p(*pairs):
        for pair in pairs:
            for k in (2 * pair, 2 * pair + 1):
                if k > 0:
                    p_copies[k].wait_recv()
                prep_right(k)

    def arrive_q(*pairs):
        for pair in pairs:
            for m in (2 * pair, 2 * pair + 1):
                if m > 0:
                    q_copies[m].wait_recv()
                prep_left(m)

    def region(step):
        pl.when(row >= 0)(step)

    done = set()

    def tiles(ppairs, pairs):
        for ppair in ppairs:
            for pair in pairs:
                if (ppair, pair) not in done:
                    first = (ppair, pair ^ 1) not in done
                    tile(pair, pair // 2, first, ppair)
                    done.add((ppair, pair))

    arrive_p(0, 1, 7)
    arrive_q(0)
    tiles((0, 1, 7), (0,))
    arrive_q(1, 2, 6)
    tiles((0, 1, 7), (1, 2, 6))
    arrive_p(2, 6, 3, 5, 4)
    arrive_q(3, 7, 4, 5)

    joined = jnp.where(lane1 < 4, qbuf[0, 12:13], -1.0)
    for m in others:
        joined = jnp.where(lax.div(lane1, 4) == m, qbuf[m, 12:13], joined)
    tbuf[0] = joined
    t_copies = {k: p_copy(tbuf.at[0], tbuf, t_recv, k, 2) for k in others}
    for k in others:
        t_copies[k].start()

    r_copies = {k: p_copy(sendr.at[k], rbuf, r_recv, k, 3, -1) for k in others}
    def finish(ppairs):
        tiles(ppairs, range(8))
        for k in (2 * p + kc for p in ppairs for kc in range(NC)):
            for mx in range(NX):
                at = pl.ds(k * W, W)
                sendr[k, 4 * mx : 4 * mx + 4] = acc[mx, 0:4, at] + (
                    acc[mx, 4:8, at] + acc[mx, 8:12, at]
                )
            if k > 0:
                r_copies[k].start()

    region(lambda: finish((4, 3, 5)))
    region(lambda: finish((2, 6)))
    region(lambda: finish((1, 7, 0)))

    for k in others:
        t_copies[k].wait_recv()

    sub16 = lax.broadcasted_iota(jnp.int32, (16, W), 0)
    lane16 = lax.broadcasted_iota(jnp.int32, (16, W), 1)
    group = lax.div(sub16, 4)
    tt = [jnp.concatenate([tbuf[2 * kz + kc] for kz in range(NZ)], 0) for kc in range(NC)]
    own = row.astype(F32)
    lists_me = sum((t == own).astype(F32) for t in tt)
    degree = lists_me + sum(
        jnp.where((t >= 0.0) & (lane < 16) & (sub == 0), 1.0, 0.0) for t in tt
    )
    degree = jnp.sum(jnp.sum(degree, axis=1, keepdims=True), axis=0, keepdims=True)
    mine = [jnp.where(lane1 < 16, t[0:1], -1.0) for t in tt]
    d = dirs[...]
    weighted = jnp.zeros((16, W), F32)
    for kz in (4, 3, 5, 2, 6, 1, 7, 0):
        at = (NZ - kz) % NZ
        block = (lax.rem(x + NX - group, NX) * NZ + lax.rem(z + kz, NZ)).astype(F32)
        linked = jnp.where(lax.div(lane16, 16) == group, lists_me[at : at + 1], 0.0)
        linked += sum((t == block).astype(F32) for t in mine)
        weight = jnp.sum(linked, axis=1, keepdims=True)
        if kz == 0:
            weight = jnp.where(sub16[:, 0:1] < 4, 1.0 + degree, weight)
        for k in (2 * kz, 2 * kz + 1):
            if k > 0:
                r_copies[k].wait_recv()
            weighted += weight * (rbuf[k] if k > 0 else sendr[0])
    image = sum(weighted[4 * mx : 4 * mx + 4] for mx in range(NX)) + noise[0] * d

    loads[5].wait()
    loads[6].wait()
    r = res[...]
    parts = jnp.concatenate([r * r, d * image, r * image, image * image], 0)
    sums = jnp.sum(parts, axis=1, keepdims=True)
    s1buf[0] = jnp.sum(jnp.where(sub16 == lane16, sums, 0.0), axis=0, keepdims=True)
    pair_copy = p_copy(s1buf.at[0], s1buf, s1_recv, 1, 4)
    pair_copy.start()
    pair_copy.wait_recv()
    s2buf[0:1] = s1buf[0] + s1buf[1]

    xs = [lax.rem(x + d, NX) * NZ for d in range(NX)]
    ys = [lax.rem(y + d, NY) * NC + core for d in range(NY)]
    zs = [lax.rem(z + d, NZ) for d in range(NZ)]

    def hops(slot):
        at = ((slot // 32, NX), (slot // 8 % 4, NY), (slot % 8, NZ))
        return sum(min(d, extent - d) for d, extent in at)

    for slot in sorted(range(1, CHIPS), key=hops, reverse=True):
        pltpu.make_async_remote_copy(
            src_ref=s2buf.at[pl.ds(0, 1)], dst_ref=s2buf.at[pl.ds(slot, 1)],
            send_sem=send_sem.at[5, 0], recv_sem=s2_recv.at[0],
            device_id=(xs[slot // 32] + zs[slot % 8], ys[slot // 8 % 4]), device_id_type=MESH,
        ).start()
    rest = s2buf.at[pl.ds(1, CHIPS - 1)]
    pltpu.make_async_copy(rest, rest, s2_recv.at[0]).wait()
    total = jnp.sum(s2buf[...], axis=0, keepdims=True)
    sums = jnp.sum(jnp.where(sub16 == lane16, total, 0.0), axis=1, keepdims=True)
    rr, curv, ri, ii = (sums[4 * i : 4 * i + 4] for i in range(4))
    alpha = rr / curv
    rr_new = jnp.maximum(rr - alpha * (2.0 * ri - alpha * ii), 0.0)
    beta = rr_new / rr
    nr = r - alpha * image
    out[0:4] = sol[...] + alpha * d
    out[4:8] = nr
    out[8:12] = nr + beta * d
    pair_copy.wait_send()
    pltpu.make_async_copy(rest, rest, send_sem.at[5, 0]).wait()
    for copies in (p_copies, q_copies, t_copies, r_copies):
        for k in others:
            copies[k].wait_send()


def local(points, length_scales, noise, tile_table, solution, residual, direction):
    hbm = pl.BlockSpec(memory_space=pltpu.HBM)
    dma = pltpu.SemaphoreType.DMA
    arrays = (length_scales, noise.reshape(1), tile_table, points, solution, residual, direction)
    out = pl.pallas_call(
        body,
        out_shape=pltpu.VMEM((12, W), F32),
        in_specs=[hbm] * 7,
        out_specs=pl.BlockSpec(memory_space=pltpu.VMEM),
        scratch_shapes=[
            pltpu.SMEM((8,), F32),
            pltpu.SMEM((1,), F32),
            pltpu.SMEM((4,), jnp.int32),
            pltpu.VMEM((8, W), F32),
            pltpu.VMEM((4, W), F32),
            pltpu.VMEM((4, W), F32),
            pltpu.VMEM((4, W), F32),
            pltpu.VMEM((GROUP, 8, W), F32),
            pltpu.VMEM((GROUP, 16, W), F32),
            pltpu.VMEM((GROUP, 1, W), F32),
            pltpu.VMEM((GROUP, 16, W), F32),
            pltpu.VMEM((2, 1, W), F32),
            pltpu.VMEM((CHIPS, W), F32),
            pltpu.VMEM((GROUP, 16, W), F32),
            pltpu.VMEM((GROUP * W, DEPTH), BF16),
            pltpu.VMEM((DEPTH, GROUP * W), BF16),
            pltpu.VMEM((16, GROUP * W), BF16),
            pltpu.VMEM((NX, 16, GROUP * W), F32),
            dma((7,)),
        ]
        + [dma((GROUP,))] * 6
        + [dma((6, GROUP))],
        compiler_params=pltpu.CompilerParams(
            collective_id=0, has_side_effects=True, vmem_limit_bytes=40 * 2**20
        ),
    )(*(a if i in (1,) else pltpu.with_memory_space_constraint(a, pltpu.HBM) for i, a in enumerate(arrays)))
    return out[0:4], out[4:8], out[8:12]


def solution(mesh):
    vec = P(None, ("row", "col"))
    return jax.shard_map(
        local,
        mesh=mesh,
        in_specs=(vec, P(), P(), P(("row", "col")), vec, vec, vec),
        out_specs=(vec, vec, vec),
        check_vma=False,
    )
```

```python
import math

import jax
import jax.numpy as jnp
from jax import lax
from jax.experimental import pallas as pl
from jax.experimental.pallas import tpu as pltpu
from jax.sharding import PartitionSpec as P

F32, BF16 = jnp.float32, jnp.bfloat16
MESH = pl.DeviceIdType.MESH
ROOT3 = math.sqrt(3.0)
RATE = -ROOT3 * math.log2(math.e)
POINT_SCALE = math.sqrt(5.0 / 3.0)
NX, NY, NZ, NC = 4, 4, 8, 2
CHIPS = NX * NY * NZ
GROUP = 16
W = 128
DEPTH = 64


def split3(a):
    high = a.astype(BF16).astype(F32)
    rest = a - high
    mid = rest.astype(BF16).astype(F32)
    return high, mid, rest - mid


def norm_rows(a, first):
    n = split3(jnp.sum(a * a, axis=0, keepdims=True))
    row = lax.broadcasted_iota(jnp.int32, a.shape, 0)
    at = 0 if first else 3
    ones = ((row >= 3 - at) & (row < 6 - at)).astype(F32)
    for k in range(3):
        ones = jnp.where(row == at + k, n[k], ones)
    return ones


def right_rows(a):
    h, m, l = split3(a)
    return jnp.concatenate([h, h, h, m, m, l, norm_rows(a, False), jnp.zeros_like(a)], 0)


def left_rows(a):
    h, m, l = (-2.0 * part for part in split3(a))
    return jnp.concatenate([h, m, l, h, m, h, norm_rows(a, True), jnp.zeros_like(a)], 0)


def kern_of(s):
    s = jnp.maximum(s, 1e-30)
    v = s * lax.rsqrt(s)
    return (s + (ROOT3 * v + 1.0)) * jnp.exp2(v * RATE)


def body(
    scales_in, noise_in, table_in, points_in, sol_in, res_in, dirs_in, out,
    scales, noise, table, points, sol, res, dirs,
    pbuf, qbuf, tbuf, rbuf, s1buf, s2buf, sendr, left, right, dlhs, acc, weights,
    in_sem, p_recv, q_recv, t_recv, r_recv, s1_recv, s2_recv, send_sem,
):
    row, col = lax.axis_index("row"), lax.axis_index("col")
    x, z = lax.div(row, NZ), lax.rem(row, NZ)
    y, core = lax.div(col, NC), lax.rem(col, NC)

    def p_at(k, sign):
        zz = lax.rem(z + (sign * (k // NC)) % NZ, NZ)
        cc = lax.rem(core + k % NC, NC)
        return (x * NZ + zz, y * NC + cc)

    def q_at(m, sign):
        xx = lax.rem(x + (sign * (m // NY)) % NX, NX)
        yy = lax.rem(y + (sign * (m % NY)) % NY, NY)
        return (xx * NZ + z, yy * NC + core)

    loads = [
        pltpu.make_async_copy(src, dst, in_sem.at[i])
        for i, (src, dst) in enumerate(
            (
                (points_in, points), (scales_in, scales), (table_in, table), (dirs_in, dirs),
                (noise_in, noise), (sol_in, sol), (res_in, res),
            )
        )
    ]
    others = range(1, GROUP)
    far_p = (8, 9, 6, 7, 10, 11, 4, 5, 12, 13, 2, 3, 14, 15, 1)
    far_q = (10, 9, 11, 6, 14, 2, 8, 5, 7, 13, 15, 1, 3, 4, 12)
    barrier = pltpu.get_barrier_semaphore()
    for k, m in zip(far_p, far_q):
        pl.semaphore_signal(barrier, inc=1, device_id=p_at(k, 1), device_id_type=MESH)
        pl.semaphore_signal(barrier, inc=1, device_id=q_at(m, 1), device_id_type=MESH)

    for load in loads:
        load.start()
    sub = lax.broadcasted_iota(jnp.int32, (8, W), 0)
    lane = lax.broadcasted_iota(jnp.int32, (8, W), 1)
    for load in loads[:5]:
        load.wait()
    col_scale = jnp.full((8, W), scales[0], F32)
    for f in range(1, 8):
        col_scale = jnp.where(sub == f, scales[f], col_scale)
    a = points[...] / col_scale * POINT_SCALE
    pbuf[0] = a
    lane1 = lax.broadcasted_iota(jnp.int32, (1, W), 1)
    own_table = jnp.full((1, W), table[0].astype(F32), F32)
    for s in range(1, 4):
        own_table = jnp.where(lax.rem(lane1, 4) == s, table[s].astype(F32), own_table)
    qbuf[0, 0:8] = a
    qbuf[0, 8:12] = dirs[...]
    qbuf[0, 12:16] = jnp.broadcast_to(own_table, (4, W))

    def p_copy(src, buf, recv, k, sem, sign=1):
        return pltpu.make_async_remote_copy(
            src_ref=src, dst_ref=buf.at[k], send_sem=send_sem.at[sem, k], recv_sem=recv.at[k],
            device_id=p_at(k, sign), device_id_type=MESH,
        )

    def q_copy(src, buf, recv, k, sem):
        return pltpu.make_async_remote_copy(
            src_ref=src, dst_ref=buf.at[k], send_sem=send_sem.at[sem, k], recv_sem=recv.at[k],
            device_id=q_at(k, 1), device_id_type=MESH,
        )

    pl.semaphore_wait(barrier, 2 * (GROUP - 1))
    p_copies = {k: p_copy(pbuf.at[0], pbuf, p_recv, k, 0) for k in others}
    q_copies = {k: q_copy(qbuf.at[0], qbuf, q_recv, k, 1) for k in others}
    for k, m in zip(far_p, far_q):
        p_copies[k].start()
        q_copies[m].start()

    def prep_right(k):
        right[:, pl.ds(k * W, W)] = right_rows(pbuf[k]).astype(BF16)

    def prep_left(m):
        left[pl.ds(m * W, W), :] = left_rows(qbuf[m, 0:8]).astype(BF16).T
        h, mid, low = split3(qbuf[m, 8:12])
        dlhs[:, pl.ds(m * W, W)] = jnp.concatenate([h, mid, low, jnp.zeros_like(h)], 0).astype(BF16)

    def tile(pair, mx, first, ppair):
        q0, p0 = pair * 256, ppair * 256
        s = jnp.dot(left[pl.ds(q0, 256), :], right[:, pl.ds(p0, 256)], preferred_element_type=F32)
        kern = kern_of(s)
        high = kern.astype(BF16)
        low = (kern - high.astype(F32)).astype(BF16)
        d = dlhs[:, pl.ds(q0, 256)]
        both = jnp.dot(d, high, preferred_element_type=F32)
        both += jnp.dot(d, low, preferred_element_type=F32)
        at = (mx, slice(None), pl.ds(p0, 256))
        acc[at] = both if first else acc[at] + both

    def arrive_p(*pairs):
        for pair in pairs:
            for k in (2 * pair, 2 * pair + 1):
                if k > 0:
                    p_copies[k].wait_recv()
                prep_right(k)

    def arrive_q(*pairs):
        for pair in pairs:
            for m in (2 * pair, 2 * pair + 1):
                if m > 0:
                    q_copies[m].wait_recv()
                prep_left(m)

    def region(step):
        pl.when(row >= 0)(step)

    done = set()

    def tiles(ppairs, pairs):
        for ppair in ppairs:
            for pair in pairs:
                if (ppair, pair) not in done:
                    first = (ppair, pair ^ 1) not in done
                    tile(pair, pair // 2, first, ppair)
                    done.add((ppair, pair))

    arrive_p(1, 7)
    arrive_q(0)
    tiles((1, 7), (0,))
    arrive_q(1, 2, 6)
    tiles((1, 7), (1, 2, 6))
    arrive_p(4, 3, 5, 2, 6, 0)
    arrive_q(3, 7, 4, 5)

    r_copies = {k: p_copy(sendr.at[k], rbuf, r_recv, k, 3, -1) for k in others}
    def finish(ppairs):
        tiles(ppairs, range(8))
        for k in (2 * p + kc for p in ppairs for kc in range(NC)):
            for mx in range(NX):
                at = pl.ds(k * W, W)
                sendr[k, 4 * mx : 4 * mx + 4] = acc[mx, 0:4, at] + (
                    acc[mx, 4:8, at] + acc[mx, 8:12, at]
                )
            if k > 0:
                r_copies[k].start()

    finish((4,))
    joined = jnp.where(lane1 < 4, qbuf[0, 12:13], -1.0)
    for m in others:
        joined = jnp.where(lax.div(lane1, 4) == m, qbuf[m, 12:13], joined)
    tbuf[0] = joined
    t_copies = {k: p_copy(tbuf.at[0], tbuf, t_recv, k, 2) for k in others}
    for k in far_p:
        t_copies[k].start()

    for ppair in (3, 5, 6, 2, 1):
        finish((ppair,))

    for k in others:
        t_copies[k].wait_recv()

    sub16 = lax.broadcasted_iota(jnp.int32, (16, W), 0)
    lane16 = lax.broadcasted_iota(jnp.int32, (16, W), 1)
    group = lax.div(sub16, 4)
    tt = [jnp.concatenate([tbuf[2 * kz + kc] for kz in range(NZ)], 0) for kc in range(NC)]
    own = row.astype(F32)
    lists_me = sum((t == own).astype(F32) for t in tt)
    degree = lists_me + sum(
        jnp.where((t >= 0.0) & (lane < 16) & (sub == 0), 1.0, 0.0) for t in tt
    )
    degree = jnp.sum(jnp.sum(degree, axis=1, keepdims=True), axis=0, keepdims=True)
    mine = [jnp.where(lane1 < 16, t[0:1], -1.0) for t in tt]
    for kz in range(NZ):
        at = (NZ - kz) % NZ
        block = (lax.rem(x + NX - group, NX) * NZ + lax.rem(z + kz, NZ)).astype(F32)
        linked = jnp.where(lax.div(lane16, 16) == group, lists_me[at : at + 1], 0.0)
        linked += sum((t == block).astype(F32) for t in mine)
        weight = jnp.sum(linked, axis=1, keepdims=True)
        if kz == 0:
            weight = jnp.where(sub16[:, 0:1] < 4, 1.0 + degree, weight)
        weights[kz] = jnp.broadcast_to(weight, (16, W))

    for ppair in (7, 0):
        finish((ppair,))


    d = dirs[...]
    weighted = jnp.zeros((16, W), F32)
    for kz in (4, 3, 5, 2, 6, 1, 7, 0):
        for k in (2 * kz, 2 * kz + 1):
            if k > 0:
                r_copies[k].wait_recv()
            weighted += weights[kz] * (rbuf[k] if k > 0 else sendr[0])
    image = sum(weighted[4 * mx : 4 * mx + 4] for mx in range(NX)) + noise[0] * d

    loads[5].wait()
    loads[6].wait()
    r = res[...]
    parts = jnp.concatenate([r * r, d * image, r * image, image * image], 0)
    sums = jnp.sum(parts, axis=1, keepdims=True)
    s1buf[0] = jnp.sum(jnp.where(sub16 == lane16, sums, 0.0), axis=0, keepdims=True)
    pair_copy = p_copy(s1buf.at[0], s1buf, s1_recv, 1, 4)
    pair_copy.start()
    pair_copy.wait_recv()
    s2buf[0:1] = s1buf[0] + s1buf[1]

    xs = [lax.rem(x + d, NX) * NZ for d in range(NX)]
    ys = [lax.rem(y + d, NY) * NC + core for d in range(NY)]
    zs = [lax.rem(z + d, NZ) for d in range(NZ)]

    def hops(slot):
        at = ((slot // 32, NX), (slot // 8 % 4, NY), (slot % 8, NZ))
        return sum(min(d, extent - d) for d, extent in at)

    for slot in sorted(range(1, CHIPS), key=hops, reverse=True):
        pltpu.make_async_remote_copy(
            src_ref=s2buf.at[pl.ds(0, 1)], dst_ref=s2buf.at[pl.ds(slot, 1)],
            send_sem=send_sem.at[5, 0], recv_sem=s2_recv.at[0],
            device_id=(xs[slot // 32] + zs[slot % 8], ys[slot // 8 % 4]), device_id_type=MESH,
        ).start()
    rest = s2buf.at[pl.ds(1, CHIPS - 1)]
    pltpu.make_async_copy(rest, rest, s2_recv.at[0]).wait()
    total = jnp.sum(s2buf[...], axis=0, keepdims=True)
    sums = jnp.sum(jnp.where(sub16 == lane16, total, 0.0), axis=1, keepdims=True)
    rr, curv, ri, ii = (sums[4 * i : 4 * i + 4] for i in range(4))
    alpha = rr / curv
    rr_new = jnp.maximum(rr - alpha * (2.0 * ri - alpha * ii), 0.0)
    beta = rr_new / rr
    nr = r - alpha * image
    out[0:4] = sol[...] + alpha * d
    out[4:8] = nr
    out[8:12] = nr + beta * d
    pair_copy.wait_send()
    pltpu.make_async_copy(rest, rest, send_sem.at[5, 0]).wait()
    for copies in (p_copies, q_copies, t_copies, r_copies):
        for k in others:
            copies[k].wait_send()


def local(points, length_scales, noise, tile_table, solution, residual, direction):
    hbm = pl.BlockSpec(memory_space=pltpu.HBM)
    dma = pltpu.SemaphoreType.DMA
    arrays = (length_scales, noise.reshape(1), tile_table, points, solution, residual, direction)
    out = pl.pallas_call(
        body,
        out_shape=pltpu.VMEM((12, W), F32),
        in_specs=[hbm] * 7,
        out_specs=pl.BlockSpec(memory_space=pltpu.VMEM),
        scratch_shapes=[
            pltpu.SMEM((8,), F32),
            pltpu.SMEM((1,), F32),
            pltpu.SMEM((4,), jnp.int32),
            pltpu.VMEM((8, W), F32),
            pltpu.VMEM((4, W), F32),
            pltpu.VMEM((4, W), F32),
            pltpu.VMEM((4, W), F32),
            pltpu.VMEM((GROUP, 8, W), F32),
            pltpu.VMEM((GROUP, 16, W), F32),
            pltpu.VMEM((GROUP, 1, W), F32),
            pltpu.VMEM((GROUP, 16, W), F32),
            pltpu.VMEM((2, 1, W), F32),
            pltpu.VMEM((CHIPS, W), F32),
            pltpu.VMEM((GROUP, 16, W), F32),
            pltpu.VMEM((GROUP * W, DEPTH), BF16),
            pltpu.VMEM((DEPTH, GROUP * W), BF16),
            pltpu.VMEM((16, GROUP * W), BF16),
            pltpu.VMEM((NX, 16, GROUP * W), F32),
            pltpu.VMEM((NZ, 16, W), F32),
            dma((7,)),
        ]
        + [dma((GROUP,))] * 6
        + [dma((6, GROUP))],
        compiler_params=pltpu.CompilerParams(
            collective_id=0, has_side_effects=True, vmem_limit_bytes=40 * 2**20
        ),
    )(*(a if i in (1,) else pltpu.with_memory_space_constraint(a, pltpu.HBM) for i, a in enumerate(arrays)))
    return out[0:4], out[4:8], out[8:12]


def solution(mesh):
    vec = P(None, ("row", "col"))
    return jax.shard_map(
        local,
        mesh=mesh,
        in_specs=(vec, P(), P(), P(("row", "col")), vec, vec, vec),
        out_specs=(vec, vec, vec),
        check_vma=False,
    )
```

```python
import math

import jax
import jax.numpy as jnp
from jax import lax
from jax.experimental import pallas as pl
from jax.experimental.pallas import tpu as pltpu
from jax.sharding import PartitionSpec as P

F32, BF16 = jnp.float32, jnp.bfloat16
MESH = pl.DeviceIdType.MESH
ROOT3 = math.sqrt(3.0)
RATE = -ROOT3 * math.log2(math.e)
POINT_SCALE = math.sqrt(5.0 / 3.0)
NX, NY, NZ, NC = 4, 4, 8, 2
CHIPS = NX * NY * NZ
P_GROUPS = ((1, 1), (2, 3), (14, 15), (4, 13))
Q_GROUPS = ((1, 1), (2, 5), (12, 13), (6, 11), (14, 15))
GROUP = 16
W = 128
DEPTH = 64


def split3(a):
    high = a.astype(BF16).astype(F32)
    rest = a - high
    mid = rest.astype(BF16).astype(F32)
    return high, mid, rest - mid


def norm_rows(a, first):
    n = split3(jnp.sum(a * a, axis=0, keepdims=True))
    row = lax.broadcasted_iota(jnp.int32, a.shape, 0)
    at = 0 if first else 3
    ones = ((row >= 3 - at) & (row < 6 - at)).astype(F32)
    for k in range(3):
        ones = jnp.where(row == at + k, n[k], ones)
    return ones


def right_rows(a):
    h, m, l = split3(a)
    return jnp.concatenate([h, h, h, m, m, l, norm_rows(a, False), jnp.zeros_like(a)], 0)


def left_rows(a):
    h, m, l = (-2.0 * part for part in split3(a))
    return jnp.concatenate([h, m, l, h, m, h, norm_rows(a, True), jnp.zeros_like(a)], 0)


def kern_of(s):
    s = jnp.maximum(s, 1e-30)
    v = s * lax.rsqrt(s)
    return (s + (ROOT3 * v + 1.0)) * jnp.exp2(v * RATE)


def body(
    scales_in, noise_in, table_in, points_in, sol_in, res_in, dirs_in, out,
    scales, noise, table, points, sol, res, dirs,
    pbuf, qbuf, tbuf, rbuf, s1buf, s2buf, sendr, left, right, dlhs, acc, weights,
    in_sem, p_recv, q_recv, t_recv, r_recv, s1_recv, s2_recv, send_sem,
):
    row, col = lax.axis_index("row"), lax.axis_index("col")
    x, z = lax.div(row, NZ), lax.rem(row, NZ)
    y, core = lax.div(col, NC), lax.rem(col, NC)

    def p_at(k, sign):
        zz = lax.rem(z + (sign * (k // NC)) % NZ, NZ)
        cc = lax.rem(core + k % NC, NC)
        return (x * NZ + zz, y * NC + cc)

    def q_at(m, sign):
        xx = lax.rem(x + (sign * (m // NY)) % NX, NX)
        yy = lax.rem(y + (sign * (m % NY)) % NY, NY)
        return (xx * NZ + z, yy * NC + core)

    loads = [
        pltpu.make_async_copy(src, dst, in_sem.at[i])
        for i, (src, dst) in enumerate(
            (
                (points_in, points), (scales_in, scales), (table_in, table), (dirs_in, dirs),
                (noise_in, noise), (sol_in, sol), (res_in, res),
            )
        )
    ]
    others = range(1, GROUP)
    far_p = (8, 9, 6, 7, 10, 11, 4, 5, 12, 13, 2, 3, 14, 15, 1)
    far_q = (10, 9, 11, 6, 14, 2, 8, 5, 7, 13, 15, 1, 3, 4, 12)
    barrier = pltpu.get_barrier_semaphore()
    for k, m in zip(far_p, far_q):
        pl.semaphore_signal(barrier, inc=1, device_id=p_at(k, 1), device_id_type=MESH)
        pl.semaphore_signal(barrier, inc=1, device_id=q_at(m, 1), device_id_type=MESH)

    for load in loads:
        load.start()
    sub = lax.broadcasted_iota(jnp.int32, (8, W), 0)
    lane = lax.broadcasted_iota(jnp.int32, (8, W), 1)
    for load in loads[:5]:
        load.wait()
    col_scale = jnp.full((8, W), scales[0], F32)
    for f in range(1, 8):
        col_scale = jnp.where(sub == f, scales[f], col_scale)
    a = points[...] / col_scale * POINT_SCALE
    pbuf[0] = a
    lane1 = lax.broadcasted_iota(jnp.int32, (1, W), 1)
    own_table = jnp.full((1, W), table[0].astype(F32), F32)
    for s in range(1, 4):
        own_table = jnp.where(lax.rem(lane1, 4) == s, table[s].astype(F32), own_table)
    qbuf[0, 0:8] = a
    qbuf[0, 8:12] = dirs[...]
    qbuf[0, 12:16] = jnp.broadcast_to(own_table, (4, W))

    groups = {id(p_recv): P_GROUPS, id(q_recv): Q_GROUPS}

    def group_of(recv, k):
        spans = groups.get(id(recv), ((1, 15),))
        return [i for i, (first, last) in enumerate(spans) if first <= k <= last][0]

    def wait_bytes(ref, sem):
        pltpu.make_async_copy(ref, ref, sem).wait()

    def arrive(buf, recv, group):
        first, last = groups.get(id(recv), ((1, 15),))[group]
        wait_bytes(buf.at[pl.ds(first, last - first + 1)], recv.at[group])

    def p_copy(src, buf, recv, k, sem, sign=1):
        return pltpu.make_async_remote_copy(
            src_ref=src, dst_ref=buf.at[k], send_sem=send_sem.at[sem], recv_sem=recv.at[group_of(recv, k)],
            device_id=p_at(k, sign), device_id_type=MESH,
        )

    def q_copy(src, buf, recv, k, sem):
        return pltpu.make_async_remote_copy(
            src_ref=src, dst_ref=buf.at[k], send_sem=send_sem.at[sem], recv_sem=recv.at[group_of(recv, k)],
            device_id=q_at(k, 1), device_id_type=MESH,
        )

    pl.semaphore_wait(barrier, 2 * (GROUP - 1))
    p_copies = {k: p_copy(pbuf.at[0], pbuf, p_recv, k, 0) for k in others}
    q_copies = {k: q_copy(qbuf.at[0], qbuf, q_recv, k, 1) for k in others}
    for k, m in zip(far_p, far_q):
        p_copies[k].start()
        q_copies[m].start()

    def prep_right(k):
        right[:, pl.ds(k * W, W)] = right_rows(pbuf[k]).astype(BF16)

    def prep_left(m):
        left[pl.ds(m * W, W), :] = left_rows(qbuf[m, 0:8]).astype(BF16).T
        h, mid, low = split3(qbuf[m, 8:12])
        dlhs[:, pl.ds(m * W, W)] = jnp.concatenate([h, mid, low, jnp.zeros_like(h)], 0).astype(BF16)

    def tile(pair, mx, first, ppair):
        q0, p0 = pair * 256, ppair * 256
        s = jnp.dot(left[pl.ds(q0, 256), :], right[:, pl.ds(p0, 256)], preferred_element_type=F32)
        kern = kern_of(s)
        high = kern.astype(BF16)
        low = (kern - high.astype(F32)).astype(BF16)
        d = dlhs[:, pl.ds(q0, 256)]
        both = jnp.dot(d, high, preferred_element_type=F32)
        both += jnp.dot(d, low, preferred_element_type=F32)
        at = (mx, slice(None), pl.ds(p0, 256))
        acc[at] = both if first else acc[at] + both

    def take_p(*pairs):
        for pair in pairs:
            for k in (2 * pair, 2 * pair + 1):
                prep_right(k)

    def take_q(*pairs):
        for pair in pairs:
            for m in (2 * pair, 2 * pair + 1):
                prep_left(m)

    def region(step):
        pl.when(row >= 0)(step)

    done = set()

    def tiles(ppairs, pairs):
        for ppair in ppairs:
            for pair in pairs:
                if (ppair, pair) not in done:
                    first = (ppair, pair ^ 1) not in done
                    tile(pair, pair // 2, first, ppair)
                    done.add((ppair, pair))

    arrive(pbuf, p_recv, 1)
    arrive(pbuf, p_recv, 2)
    take_p(1, 7)
    arrive(qbuf, q_recv, 0)
    take_q(0)
    tiles((1, 7), (0,))
    arrive(qbuf, q_recv, 1)
    arrive(qbuf, q_recv, 2)
    take_q(1, 2, 6)
    tiles((1, 7), (1, 2, 6))
    arrive(pbuf, p_recv, 0)
    arrive(pbuf, p_recv, 3)
    take_p(4, 3, 5, 2, 6, 0)
    arrive(qbuf, q_recv, 3)
    arrive(qbuf, q_recv, 4)
    take_q(3, 7, 4, 5)

    r_copies = {k: p_copy(sendr.at[k], rbuf, r_recv, k, 3, -1) for k in others}
    def finish(ppairs):
        tiles(ppairs, range(8))
        for k in (2 * p + kc for p in ppairs for kc in range(NC)):
            for mx in range(NX):
                at = pl.ds(k * W, W)
                sendr[k, 4 * mx : 4 * mx + 4] = acc[mx, 0:4, at] + (
                    acc[mx, 4:8, at] + acc[mx, 8:12, at]
                )
            if k > 0:
                r_copies[k].start()

    finish((4,))
    joined = jnp.where(lane1 < 4, qbuf[0, 12:13], -1.0)
    for m in others:
        joined = jnp.where(lax.div(lane1, 4) == m, qbuf[m, 12:13], joined)
    tbuf[0] = joined
    t_copies = {k: p_copy(tbuf.at[0], tbuf, t_recv, k, 2) for k in others}
    for k in far_p:
        t_copies[k].start()

    for ppair in (3, 5, 6, 2, 1):
        finish((ppair,))

    arrive(tbuf, t_recv, 0)

    sub16 = lax.broadcasted_iota(jnp.int32, (16, W), 0)
    lane16 = lax.broadcasted_iota(jnp.int32, (16, W), 1)
    group = lax.div(sub16, 4)
    tt = [jnp.concatenate([tbuf[2 * kz + kc] for kz in range(NZ)], 0) for kc in range(NC)]
    own = row.astype(F32)
    lists_me = sum((t == own).astype(F32) for t in tt)
    degree = lists_me + sum(
        jnp.where((t >= 0.0) & (lane < 16) & (sub == 0), 1.0, 0.0) for t in tt
    )
    degree = jnp.sum(jnp.sum(degree, axis=1, keepdims=True), axis=0, keepdims=True)
    mine = [jnp.where(lane1 < 16, t[0:1], -1.0) for t in tt]
    for kz in range(NZ):
        at = (NZ - kz) % NZ
        block = (lax.rem(x + NX - group, NX) * NZ + lax.rem(z + kz, NZ)).astype(F32)
        linked = jnp.where(lax.div(lane16, 16) == group, lists_me[at : at + 1], 0.0)
        linked += sum((t == block).astype(F32) for t in mine)
        weight = jnp.sum(linked, axis=1, keepdims=True)
        if kz == 0:
            weight = jnp.where(sub16[:, 0:1] < 4, 1.0 + degree, weight)
        weights[kz] = jnp.broadcast_to(weight, (16, W))

    for ppair in (7, 0):
        finish((ppair,))


    d = dirs[...]
    arrive(rbuf, r_recv, 0)
    weighted = jnp.zeros((16, W), F32)
    for kz in (4, 3, 5, 2, 6, 1, 7, 0):
        for k in (2 * kz, 2 * kz + 1):
            weighted += weights[kz] * (rbuf[k] if k > 0 else sendr[0])
    image = sum(weighted[4 * mx : 4 * mx + 4] for mx in range(NX)) + noise[0] * d

    loads[5].wait()
    loads[6].wait()
    r = res[...]
    parts = jnp.concatenate([r * r, d * image, r * image, image * image], 0)
    sums = jnp.sum(parts, axis=1, keepdims=True)
    s1buf[0] = jnp.sum(jnp.where(sub16 == lane16, sums, 0.0), axis=0, keepdims=True)
    pair_copy = p_copy(s1buf.at[0], s1buf, s1_recv, 1, 4)
    pair_copy.start()
    pair_copy.wait_recv()
    s2buf[0:1] = s1buf[0] + s1buf[1]

    xs = [lax.rem(x + d, NX) * NZ for d in range(NX)]
    ys = [lax.rem(y + d, NY) * NC + core for d in range(NY)]
    zs = [lax.rem(z + d, NZ) for d in range(NZ)]

    def hops(slot):
        at = ((slot // 32, NX), (slot // 8 % 4, NY), (slot % 8, NZ))
        return sum(min(d, extent - d) for d, extent in at)

    for slot in sorted(range(1, CHIPS), key=hops, reverse=True):
        pltpu.make_async_remote_copy(
            src_ref=s2buf.at[pl.ds(0, 1)], dst_ref=s2buf.at[pl.ds(slot, 1)],
            send_sem=send_sem.at[5], recv_sem=s2_recv.at[0],
            device_id=(xs[slot // 32] + zs[slot % 8], ys[slot // 8 % 4]), device_id_type=MESH,
        ).start()
    rest = s2buf.at[pl.ds(1, CHIPS - 1)]
    pair_copy.wait_send()
    for phase, buf in enumerate((pbuf, qbuf, tbuf, rbuf)):
        wait_bytes(buf.at[pl.ds(1, GROUP - 1)], send_sem.at[phase])
    wait_bytes(rest, send_sem.at[5])
    wait_bytes(rest, s2_recv.at[0])
    total = jnp.sum(s2buf[...], axis=0, keepdims=True)
    sums = jnp.sum(jnp.where(sub16 == lane16, total, 0.0), axis=1, keepdims=True)
    rr, curv, ri, ii = (sums[4 * i : 4 * i + 4] for i in range(4))
    alpha = rr / curv
    rr_new = jnp.maximum(rr - alpha * (2.0 * ri - alpha * ii), 0.0)
    beta = rr_new / rr
    nr = r - alpha * image
    out[0:4] = sol[...] + alpha * d
    out[4:8] = nr
    out[8:12] = nr + beta * d


def local(points, length_scales, noise, tile_table, solution, residual, direction):
    hbm = pl.BlockSpec(memory_space=pltpu.HBM)
    dma = pltpu.SemaphoreType.DMA
    arrays = (length_scales, noise.reshape(1), tile_table, points, solution, residual, direction)
    out = pl.pallas_call(
        body,
        out_shape=pltpu.VMEM((12, W), F32),
        in_specs=[hbm] * 7,
        out_specs=pl.BlockSpec(memory_space=pltpu.VMEM),
        scratch_shapes=[
            pltpu.SMEM((8,), F32),
            pltpu.SMEM((1,), F32),
            pltpu.SMEM((4,), jnp.int32),
            pltpu.VMEM((8, W), F32),
            pltpu.VMEM((4, W), F32),
            pltpu.VMEM((4, W), F32),
            pltpu.VMEM((4, W), F32),
            pltpu.VMEM((GROUP, 8, W), F32),
            pltpu.VMEM((GROUP, 16, W), F32),
            pltpu.VMEM((GROUP, 1, W), F32),
            pltpu.VMEM((GROUP, 16, W), F32),
            pltpu.VMEM((2, 1, W), F32),
            pltpu.VMEM((CHIPS, W), F32),
            pltpu.VMEM((GROUP, 16, W), F32),
            pltpu.VMEM((GROUP * W, DEPTH), BF16),
            pltpu.VMEM((DEPTH, GROUP * W), BF16),
            pltpu.VMEM((16, GROUP * W), BF16),
            pltpu.VMEM((NX, 16, GROUP * W), F32),
            pltpu.VMEM((NZ, 16, W), F32),
            dma((7,)),
        ]
        + [dma((GROUP,))] * 6
        + [dma((6,))],
        compiler_params=pltpu.CompilerParams(
            collective_id=0, has_side_effects=True, vmem_limit_bytes=40 * 2**20
        ),
    )(*(a if i in (1,) else pltpu.with_memory_space_constraint(a, pltpu.HBM) for i, a in enumerate(arrays)))
    return out[0:4], out[4:8], out[8:12]


def solution(mesh):
    vec = P(None, ("row", "col"))
    return jax.shard_map(
        local,
        mesh=mesh,
        in_specs=(vec, P(), P(), P(("row", "col")), vec, vec, vec),
        out_specs=(vec, vec, vec),
        check_vma=False,
    )
```

```python
import math

import jax
import jax.numpy as jnp
from jax import lax
from jax.experimental import pallas as pl
from jax.experimental.pallas import tpu as pltpu
from jax.sharding import PartitionSpec as P

F32, BF16 = jnp.float32, jnp.bfloat16
MESH = pl.DeviceIdType.MESH
ROOT3 = math.sqrt(3.0)
RATE = -ROOT3 * math.log2(math.e)
POINT_SCALE = math.sqrt(5.0 / 3.0)
NX, NY, NZ, NC = 4, 4, 8, 2
CHIPS = NX * NY * NZ
P_GROUPS = ((1, 1), (2, 3), (14, 15), (4, 13))
Q_GROUPS = ((1, 1), (2, 5), (12, 13), (6, 11), (14, 15))
GROUP = 16
W = 128
DEPTH = 64


def split3(a):
    high = a.astype(BF16).astype(F32)
    rest = a - high
    mid = rest.astype(BF16).astype(F32)
    return high, mid, rest - mid


def rows_of(values):
    row = lax.broadcasted_iota(jnp.int32, (8, W), 0)
    out = jnp.zeros((8, W), F32)
    for k, value in values.items():
        out = jnp.where(row == k, value, out)
    return out


def split_norm(a):
    return split3(jnp.sum(a * a, axis=0, keepdims=True))


def right_rows(a):
    h, m, l = split3(a)
    norm = rows_of(dict(enumerate(split_norm(a))))
    return jnp.concatenate([h, h, h, m, m, l, rows_of({4: 1.0, 5: 1.0, 6: 1.0}), norm], 0)


def left_rows(a, half):
    h, m, l = (-2.0 * part for part in split3(a))
    return jnp.concatenate([h, m, l, h, m, h, half, rows_of({0: 1.0, 1: 1.0, 2: 1.0})], 0)


def kern_of(s):
    s = jnp.maximum(s, 1e-30)
    v = s * lax.rsqrt(s)
    return (s + (ROOT3 * v + 1.0)) * jnp.exp2(v * RATE)


def body(
    scales_in, noise_in, table_in, points_in, sol_in, res_in, dirs_in, out,
    scales, noise, table, points, sol, res, dirs,
    pbuf, qbuf, tbuf, rbuf, s1buf, s2buf, sendr, left, right, dlhs, acc, weights,
    in_sem, p_recv, q_recv, t_recv, r_recv, s1_recv, s2_recv, send_sem,
):
    row, col = lax.axis_index("row"), lax.axis_index("col")
    x, z = lax.div(row, NZ), lax.rem(row, NZ)
    y, core = lax.div(col, NC), lax.rem(col, NC)

    def p_at(k, sign):
        zz = lax.rem(z + (sign * (k // NC)) % NZ, NZ)
        cc = lax.rem(core + k % NC, NC)
        return (x * NZ + zz, y * NC + cc)

    def q_at(m, sign):
        xx = lax.rem(x + (sign * (m // NY)) % NX, NX)
        yy = lax.rem(y + (sign * (m % NY)) % NY, NY)
        return (xx * NZ + z, yy * NC + core)

    loads = [
        pltpu.make_async_copy(src, dst, in_sem.at[i])
        for i, (src, dst) in enumerate(
            (
                (points_in, points), (scales_in, scales), (table_in, table), (dirs_in, dirs),
                (noise_in, noise), (sol_in, sol), (res_in, res),
            )
        )
    ]
    others = range(1, GROUP)
    far_p = (8, 9, 6, 7, 10, 11, 4, 5, 12, 13, 2, 3, 14, 15, 1)
    far_q = (10, 9, 11, 6, 14, 2, 8, 5, 7, 13, 15, 1, 3, 4, 12)
    barrier = pltpu.get_barrier_semaphore()
    for k, m in zip(far_p, far_q):
        pl.semaphore_signal(barrier, inc=1, device_id=p_at(k, 1), device_id_type=MESH)
        pl.semaphore_signal(barrier, inc=1, device_id=q_at(m, 1), device_id_type=MESH)

    for load in loads:
        load.start()
    sub = lax.broadcasted_iota(jnp.int32, (8, W), 0)
    lane = lax.broadcasted_iota(jnp.int32, (8, W), 1)
    for load in loads[:5]:
        load.wait()
    col_scale = jnp.full((8, W), scales[0], F32)
    for f in range(1, 8):
        col_scale = jnp.where(sub == f, scales[f], col_scale)
    a = points[...] / col_scale * POINT_SCALE
    pbuf[0] = a
    lane1 = lax.broadcasted_iota(jnp.int32, (1, W), 1)
    own_table = jnp.full((1, W), table[0].astype(F32), F32)
    for s in range(1, 4):
        own_table = jnp.where(lax.rem(lane1, 4) == s, table[s].astype(F32), own_table)
    qbuf[0, 0:8] = a
    qbuf[0, 8:12] = dirs[...]
    for k, part in enumerate(split_norm(a)):
        qbuf[0, 12 + k : 13 + k] = part
    qbuf[0, 15:16] = own_table

    groups = {id(p_recv): P_GROUPS, id(q_recv): Q_GROUPS}

    def group_of(recv, k):
        spans = groups.get(id(recv), ((1, 15),))
        return [i for i, (first, last) in enumerate(spans) if first <= k <= last][0]

    def wait_bytes(ref, sem):
        pltpu.make_async_copy(ref, ref, sem).wait()

    def arrive(buf, recv, group):
        first, last = groups.get(id(recv), ((1, 15),))[group]
        wait_bytes(buf.at[pl.ds(first, last - first + 1)], recv.at[group])

    def p_copy(src, buf, recv, k, sem, sign=1):
        return pltpu.make_async_remote_copy(
            src_ref=src, dst_ref=buf.at[k], send_sem=send_sem.at[sem], recv_sem=recv.at[group_of(recv, k)],
            device_id=p_at(k, sign), device_id_type=MESH,
        )

    def q_copy(src, buf, recv, k, sem):
        return pltpu.make_async_remote_copy(
            src_ref=src, dst_ref=buf.at[k], send_sem=send_sem.at[sem], recv_sem=recv.at[group_of(recv, k)],
            device_id=q_at(k, 1), device_id_type=MESH,
        )

    pl.semaphore_wait(barrier, 2 * (GROUP - 1))
    p_copies = {k: p_copy(pbuf.at[0], pbuf, p_recv, k, 0) for k in others}
    q_copies = {k: q_copy(qbuf.at[0], qbuf, q_recv, k, 1) for k in others}
    for k, m in zip(far_p, far_q):
        p_copies[k].start()
        q_copies[m].start()

    def prep_right(k):
        right[:, pl.ds(k * W, W)] = right_rows(pbuf[k]).astype(BF16)

    def prep_left(m):
        left[pl.ds(m * W, W), :] = left_rows(qbuf[m, 0:8], qbuf[m, 8:16]).astype(BF16).T
        h, mid, low = split3(qbuf[m, 8:12])
        dlhs[:, pl.ds(m * W, W)] = jnp.concatenate([h, mid, low, jnp.zeros_like(h)], 0).astype(BF16)

    def tile(pair, mx, first, ppair):
        add_tiles((pair,), mx, first, ppair)

    def add_tiles(pairs, mx, first, ppair):
        p0 = ppair * 256
        both = None
        for q0 in (pair * 256 for pair in pairs):
            s = jnp.dot(left[pl.ds(q0, 256), :], right[:, pl.ds(p0, 256)], preferred_element_type=F32)
            kern = kern_of(s)
            high = kern.astype(BF16)
            low = (kern - high.astype(F32)).astype(BF16)
            d = dlhs[:, pl.ds(q0, 256)]
            part = jnp.dot(d, high, preferred_element_type=F32)
            part += jnp.dot(d, low, preferred_element_type=F32)
            both = part if both is None else both + part
        at = (mx, slice(None), pl.ds(p0, 256))
        acc[at] = both if first else acc[at] + both

    def take_p(*pairs):
        for pair in pairs:
            for k in (2 * pair, 2 * pair + 1):
                prep_right(k)

    def take_q(*pairs):
        for pair in pairs:
            for m in (2 * pair, 2 * pair + 1):
                prep_left(m)

    def region(step):
        pl.when(row >= 0)(step)

    done = set()

    def tiles(ppairs, pairs):
        for ppair in ppairs:
            for pair in pairs:
                if pair % 2 == 0 and pair + 1 in pairs and not {(ppair, pair), (ppair, pair + 1)} & done:
                    add_tiles((pair, pair + 1), pair // 2, True, ppair)
                    done.update({(ppair, pair), (ppair, pair + 1)})
                if (ppair, pair) not in done:
                    first = (ppair, pair ^ 1) not in done
                    tile(pair, pair // 2, first, ppair)
                    done.add((ppair, pair))

    arrive(pbuf, p_recv, 1)
    arrive(pbuf, p_recv, 2)
    take_p(1, 7)
    arrive(qbuf, q_recv, 0)
    take_q(0)
    tiles((1, 7), (0,))
    arrive(qbuf, q_recv, 1)
    arrive(qbuf, q_recv, 2)
    take_q(1, 2, 6)
    tiles((1, 7), (1, 2, 6))
    arrive(pbuf, p_recv, 0)
    arrive(pbuf, p_recv, 3)
    take_p(4, 3, 5, 2, 6, 0)
    arrive(qbuf, q_recv, 3)
    arrive(qbuf, q_recv, 4)
    take_q(3, 7, 4, 5)

    r_copies = {k: p_copy(sendr.at[k], rbuf, r_recv, k, 3, -1) for k in others}
    def finish(ppairs):
        tiles(ppairs, range(8))
        for k in (2 * p + kc for p in ppairs for kc in range(NC)):
            for mx in range(NX):
                at = pl.ds(k * W, W)
                sendr[k, 4 * mx : 4 * mx + 4] = acc[mx, 0:4, at] + (
                    acc[mx, 4:8, at] + acc[mx, 8:12, at]
                )
            if k > 0:
                r_copies[k].start()

    finish((4,))
    joined = jnp.where(lane1 < 4, qbuf[0, 15:16], -1.0)
    for m in others:
        joined = jnp.where(lax.div(lane1, 4) == m, qbuf[m, 15:16], joined)
    tbuf[0] = joined
    t_copies = {k: p_copy(tbuf.at[0], tbuf, t_recv, k, 2) for k in others}
    for k in far_p:
        t_copies[k].start()

    for ppair in (3, 5, 6, 2, 1):
        finish((ppair,))

    for ppair in (7, 0):
        finish((ppair,))

    arrive(tbuf, t_recv, 0)

    sub16 = lax.broadcasted_iota(jnp.int32, (16, W), 0)
    lane16 = lax.broadcasted_iota(jnp.int32, (16, W), 1)
    group = lax.div(sub16, 4)
    tt = [jnp.concatenate([tbuf[2 * kz + kc] for kz in range(NZ)], 0) for kc in range(NC)]
    own = row.astype(F32)
    lists_me = sum((t == own).astype(F32) for t in tt)
    degree = lists_me + sum(
        jnp.where((t >= 0.0) & (lane < 16) & (sub == 0), 1.0, 0.0) for t in tt
    )
    degree = jnp.sum(jnp.sum(degree, axis=1, keepdims=True), axis=0, keepdims=True)
    mine = [jnp.where(lane1 < 16, t[0:1], -1.0) for t in tt]
    for kz in range(NZ):
        at = (NZ - kz) % NZ
        block = (lax.rem(x + NX - group, NX) * NZ + lax.rem(z + kz, NZ)).astype(F32)
        linked = jnp.where(lax.div(lane16, 16) == group, lists_me[at : at + 1], 0.0)
        linked += sum((t == block).astype(F32) for t in mine)
        weight = jnp.sum(linked, axis=1, keepdims=True)
        if kz == 0:
            weight = jnp.where(sub16[:, 0:1] < 4, 1.0 + degree, weight)
        weights[kz] = jnp.broadcast_to(weight, (16, W))


    d = dirs[...]
    arrive(rbuf, r_recv, 0)
    weighted = jnp.zeros((16, W), F32)
    for kz in (4, 3, 5, 2, 6, 1, 7, 0):
        for k in (2 * kz, 2 * kz + 1):
            weighted += weights[kz] * (rbuf[k] if k > 0 else sendr[0])
    image = sum(weighted[4 * mx : 4 * mx + 4] for mx in range(NX)) + noise[0] * d

    loads[5].wait()
    loads[6].wait()
    r = res[...]
    parts = jnp.concatenate([r * r, d * image, r * image, image * image], 0)
    sums = jnp.sum(parts, axis=1, keepdims=True)
    s1buf[0] = jnp.sum(jnp.where(sub16 == lane16, sums, 0.0), axis=0, keepdims=True)
    pair_copy = p_copy(s1buf.at[0], s1buf, s1_recv, 1, 4)
    pair_copy.start()
    pair_copy.wait_recv()
    s2buf[0:1] = s1buf[0] + s1buf[1]

    xs = [lax.rem(x + d, NX) * NZ for d in range(NX)]
    ys = [lax.rem(y + d, NY) * NC + core for d in range(NY)]
    zs = [lax.rem(z + d, NZ) for d in range(NZ)]

    def hops(slot):
        at = ((slot // 32, NX), (slot // 8 % 4, NY), (slot % 8, NZ))
        return sum(min(d, extent - d) for d, extent in at)

    for slot in sorted(range(1, CHIPS), key=hops, reverse=True):
        pltpu.make_async_remote_copy(
            src_ref=s2buf.at[pl.ds(0, 1)], dst_ref=s2buf.at[pl.ds(slot, 1)],
            send_sem=send_sem.at[5], recv_sem=s2_recv.at[0],
            device_id=(xs[slot // 32] + zs[slot % 8], ys[slot // 8 % 4]), device_id_type=MESH,
        ).start()
    rest = s2buf.at[pl.ds(1, CHIPS - 1)]
    pair_copy.wait_send()
    for phase, buf in enumerate((pbuf, qbuf, tbuf, rbuf)):
        wait_bytes(buf.at[pl.ds(1, GROUP - 1)], send_sem.at[phase])
    wait_bytes(rest, send_sem.at[5])
    wait_bytes(rest, s2_recv.at[0])
    total = jnp.sum(s2buf[...], axis=0, keepdims=True)
    sums = jnp.sum(jnp.where(sub16 == lane16, total, 0.0), axis=1, keepdims=True)
    rr, curv, ri, ii = (sums[4 * i : 4 * i + 4] for i in range(4))
    alpha = rr / curv
    rr_new = jnp.maximum(rr - alpha * (2.0 * ri - alpha * ii), 0.0)
    beta = rr_new / rr
    nr = r - alpha * image
    out[0:4] = sol[...] + alpha * d
    out[4:8] = nr
    out[8:12] = nr + beta * d


def local(points, length_scales, noise, tile_table, solution, residual, direction):
    hbm = pl.BlockSpec(memory_space=pltpu.HBM)
    dma = pltpu.SemaphoreType.DMA
    arrays = (length_scales, noise.reshape(1), tile_table, points, solution, residual, direction)
    out = pl.pallas_call(
        body,
        out_shape=pltpu.VMEM((12, W), F32),
        in_specs=[hbm] * 7,
        out_specs=pl.BlockSpec(memory_space=pltpu.VMEM),
        scratch_shapes=[
            pltpu.SMEM((8,), F32),
            pltpu.SMEM((1,), F32),
            pltpu.SMEM((4,), jnp.int32),
            pltpu.VMEM((8, W), F32),
            pltpu.VMEM((4, W), F32),
            pltpu.VMEM((4, W), F32),
            pltpu.VMEM((4, W), F32),
            pltpu.VMEM((GROUP, 8, W), F32),
            pltpu.VMEM((GROUP, 16, W), F32),
            pltpu.VMEM((GROUP, 1, W), F32),
            pltpu.VMEM((GROUP, 16, W), F32),
            pltpu.VMEM((2, 1, W), F32),
            pltpu.VMEM((CHIPS, W), F32),
            pltpu.VMEM((GROUP, 16, W), F32),
            pltpu.VMEM((GROUP * W, DEPTH), BF16),
            pltpu.VMEM((DEPTH, GROUP * W), BF16),
            pltpu.VMEM((16, GROUP * W), BF16),
            pltpu.VMEM((NX, 16, GROUP * W), F32),
            pltpu.VMEM((NZ, 16, W), F32),
            dma((7,)),
        ]
        + [dma((GROUP,))] * 6
        + [dma((6,))],
        compiler_params=pltpu.CompilerParams(
            collective_id=0, has_side_effects=True, vmem_limit_bytes=40 * 2**20
        ),
    )(*(a if i in (1,) else pltpu.with_memory_space_constraint(a, pltpu.HBM) for i, a in enumerate(arrays)))
    return out[0:4], out[4:8], out[8:12]


def solution(mesh):
    vec = P(None, ("row", "col"))
    return jax.shard_map(
        local,
        mesh=mesh,
        in_specs=(vec, P(), P(), P(("row", "col")), vec, vec, vec),
        out_specs=(vec, vec, vec),
        check_vma=False,
    )
```
